32 devices in a mesh: replica: 4 (over z), dp: 2 (over x), tensor: 4 (over y, core).
Axes of the slice: x: 2, y: 2, z: 4, core: 2. Of those that a mesh axis runs over, the one named last changes fastest.
Arguments:
- tokens: bfloat16 [4, 2048, 2048], P('replica', 'dp', 'tensor'), may hold values from -6 to 6
- grad_out: bfloat16 [4, 2048, 14336], P('replica', 'dp', 'tensor'), may hold values from -250 to 250, as said below
- weights: bfloat16 [4, 2048, 14336], P('replica', 'dp', 'tensor'), may hold values from -6 to 6
- first_moment: bfloat16 [4, 2048, 14336], P('replica', 'dp', 'tensor'), may hold values from -4 to 4
- second_moment: bfloat16 [4, 2048, 14336], P('replica', 'dp', 'tensor'), may hold values from 0.019897461 to 0.19921875
Outputs:
- new_weights: bfloat16 [4, 2048, 14336], P('replica', 'dp', 'tensor')
- new_first: bfloat16 [4, 2048, 14336], P('replica', 'dp', 'tensor')
- new_second: bfloat16 [4, 2048, 14336], P('replica', 'dp', 'tensor')
The draws below stay inside these ranges and needn't reach their ends.
Inputs may be any that keep to these rules, and one draw needn't show every extreme that they name: `grad_out`: the upstream gradient.
All inputs are finite; a program needn't handle non-finite values.
Results may differ from the reference program's by a relative error of at most 0.0051.
Values may be sent and summed in bfloat16 or wider, within the bound.
A program may use at most 192 MiB of HBM per device.

```python
import math
import jax
import jax.numpy as jnp
from jax import lax

D = 2048
FF = 14336
TOK_DEV = 1024
STEP = 1
ROWS = 2048
N_REPLICA = 4
N_DP = 2


def draw_grad_out(key, part):
    key = jax.random.fold_in(key, 7)
    key_base, key_cols, key_rows, key_pick = jax.random.split(key, 4)
    shape = (N_REPLICA, N_DP * TOK_DEV, FF)
    position = jnp.arange(FF, dtype=jnp.float32) / FF
    jitter = jax.random.uniform(key_cols, (FF,), jnp.float32, math.log(0.7), math.log(1.4))
    col_scale = jnp.exp(math.log(10.0) * position + jitter)
    order = jax.random.permutation(key_pick, N_REPLICA)
    quiet = order < max(1, N_REPLICA // 4)
    group_scale = jnp.where(quiet, 0.01 / math.sqrt(N_DP * TOK_DEV), 1.0).astype(jnp.float32)[:, None, None]
    base = jnp.clip(jax.random.normal(key_base, shape, jnp.float32), -4.0, 4.0)
    row_scale = jnp.exp(jax.random.uniform(key_rows, (N_REPLICA, N_DP * TOK_DEV, 1), jnp.float32, 0.0, math.log(3.0)))
    return (base * row_scale * col_scale[None, None, :] * group_scale).astype(jnp.bfloat16)


def shard_levels(own_key, shape, cuts, least, largest):
    loudness, own = 1.0, jax.random.fold_in(own_key, 6)
    for dim, parts in cuts:
        heights = jnp.exp(jax.random.uniform(jax.random.fold_in(own, dim), (parts,), jnp.float32, least / len(cuts), largest / len(cuts)))
        loudness = loudness * jnp.repeat(heights, shape[dim] // parts).reshape([-1 if axis == dim else 1 for axis in range(len(shape))])
    return loudness


def centred(own_key, extent, scale, reach, cuts=(), kind=jnp.bfloat16):
    entries = scale * jax.random.normal(own_key, extent, jnp.float32)
    if cuts:
        entries = entries * shard_levels(own_key, extent, cuts, -0.22, 0.18)
    return jnp.clip(entries, -reach, reach).astype(kind)


def setup_inputs(seed: int = 0) -> dict:
    key_of = jax.random.split(jax.random.key(seed), 6)
    return {
        "tokens": centred(key_of[0], (N_REPLICA, ROWS, D), 1.0, 6.0, ((0, 4), (1, 2), (2, 4))),
        "grad_out": draw_grad_out(jax.random.fold_in(key_of[5], 71), 0),
        "weights": centred(key_of[2], (N_REPLICA, D, FF), 1.0, 6.0, ((0, 4), (1, 2), (2, 4))),
        "first_moment": centred(key_of[3], (N_REPLICA, D, FF), 0.3, 4.0, ((0, 4), (1, 2), (2, 4))),
        "second_moment": jnp.clip(jnp.exp(math.log(0.19921875) - 2.3038113 * jax.random.uniform(key_of[4], (N_REPLICA, D, FF), jnp.float32) ** shard_levels(key_of[4], (N_REPLICA, D, FF), ((0, 4), (1, 2), (2, 4)), -0.2, 0.2)), 0.019897461, 0.19921875).astype(jnp.bfloat16),
    }


def adamw(grad, total, weights, first_moment, second_moment):
    clip = jnp.minimum(1.0, 1.0 / jnp.sqrt(total / (D * FF) + 1e-06))
    scaled = clip * grad
    moment_one = 0.9 * first_moment.astype(jnp.float32) + 0.1 * scaled
    moment_two = 0.95 * second_moment.astype(jnp.float32) + 0.05 * scaled * scaled
    fix_one = 1.0 - 0.9 ** STEP
    fix_two = 1.0 - 0.95 ** STEP
    update = moment_one / fix_one / (jnp.sqrt(moment_two / fix_two) + 1e-08)
    old = weights.astype(jnp.float32)
    fresh = old - 0.05 * (update + 0.1 * old)
    return jnp.stack([fresh.astype(jnp.bfloat16), moment_one.astype(jnp.bfloat16), moment_two.astype(jnp.bfloat16)])

def reference(tokens, grad_out, weights, first_moment, second_moment):

    def one_group(item):
        inputs, upstream, params, moment_one, moment_two = item
        grad = jnp.dot(inputs.T, upstream, preferred_element_type=jnp.float32)
        total = jnp.sum(grad * grad)
        return adamw(grad, total, params, moment_one, moment_two)
    states = lax.map(one_group, (tokens, grad_out, weights, first_moment, second_moment))
    partner = jnp.roll(states, N_REPLICA // 2, axis=0)
    mixed = (0.5 * (states.astype(jnp.float32) + partner.astype(jnp.float32))).astype(jnp.bfloat16)
    return (mixed[:, 0], mixed[:, 1], mixed[:, 2])
```

```python
import functools

import jax
import jax.numpy as jnp
from jax import lax
from jax.experimental import pallas as pl
from jax.experimental.pallas import tpu as pltpu
from jax.sharding import PartitionSpec as P

D = 2048
FF = 14336
STEP = 1
FIX_ONE = 1.0 - 0.9**STEP
FIX_TWO = 1.0 - 0.95**STEP
TILE = 32
SHARES = (8, 5, 2, 1)


def partner(value, axis, bit):
    mask = 2**bit
    pairs = [(source, source ^ mask) for source in range(lax.axis_size(axis))]
    return lax.ppermute(value, axis, pairs)


def second_kernel(clip_ref, grad_ref, second_ref, after_ref, out_ref):
    scaled = clip_ref[0, 0] * grad_ref[...]
    fresh = 0.95 * second_ref[...].astype(jnp.float32) + 0.05 * scaled * scaled
    out_ref[...] = fresh.astype(jnp.bfloat16)


def second_chunk(clip, grad, second, after, start, rows):
    cols = grad.shape[1]
    first = start // TILE
    return pl.pallas_call(
        second_kernel,
        grid=(rows // TILE,),
        in_specs=[
            pl.BlockSpec(memory_space=pltpu.SMEM),
            pl.BlockSpec((TILE, cols), lambda i: (first + i, 0)),
            pl.BlockSpec((TILE, cols), lambda i: (first + i, 0)),
            pl.BlockSpec(memory_space=pl.ANY),
        ],
        out_specs=pl.BlockSpec((TILE, cols), lambda i: (i, 0)),
        out_shape=jax.ShapeDtypeStruct((rows, cols), jnp.bfloat16),
        cost_estimate=pl.CostEstimate(
            flops=6 * rows * cols, bytes_accessed=8 * rows * cols, transcendentals=0
        ),
        compiler_params=pltpu.CompilerParams(vmem_limit_bytes=60 * 2**20),
    )(clip, grad, second, after)


def new_weights(old, first, second):
    old = old.astype(jnp.float32)
    first = first.astype(jnp.float32)
    second = second.astype(jnp.float32)
    update = first / FIX_ONE / (jnp.sqrt(second / FIX_TWO) + 1e-08)
    fresh = old - 0.05 * (update + 0.1 * old)
    return fresh.astype(jnp.bfloat16)


def mean(one, two):
    return (0.5 * (one.astype(jnp.float32) + two.astype(jnp.float32))).astype(jnp.bfloat16)


def mix_kernel(w, w2, m, m2, v, v2, *refs):
    out_w, out_m, out_v = refs[-3:]
    first, first2 = m[...], m2[...]
    second, second2 = v[...], v2[...]
    out_m[...] = mean(first, first2)
    out_v[...] = mean(second, second2)
    out_w[...] = mean(
        new_weights(w[...], first, second), new_weights(w2[...], first2, second2)
    )


def mix_chunk(w, w2, m, m2, v, v2, held, start):
    rows, cols = v.shape
    first = start // TILE
    far = pl.BlockSpec((TILE, cols), lambda i: (first + i, 0))
    near = pl.BlockSpec((TILE, cols), lambda i: (i, 0))
    held = tuple(held)
    return pl.pallas_call(
        mix_kernel,
        grid=(rows // TILE,),
        in_specs=[far, far, far, far, near, near] + [pl.BlockSpec(memory_space=pl.ANY)] * len(held),
        out_specs=(far, far, far),
        out_shape=(jax.ShapeDtypeStruct(w.shape, jnp.bfloat16),) * 3,
        input_output_aliases={6 + i: i for i in range(len(held))},
        cost_estimate=pl.CostEstimate(
            flops=30 * rows * cols, bytes_accessed=18 * rows * cols, transcendentals=4 * rows * cols
        ),
        compiler_params=pltpu.CompilerParams(vmem_limit_bytes=60 * 2**20),
    )(w, w2, m, m2, v, v2, *held)


def contract(one, two):
    return lax.dot_general(one, two, (((0,), (0,)), ((), ())), preferred_element_type=jnp.float32)


def body(tokens, grad_out, weights, first_moment, second_moment):
    bit = lax.axis_size("replica").bit_length() - 2
    weights, upstream = weights[0], grad_out[0]
    first_moment, second_moment = first_moment[0], second_moment[0]
    rows = weights.shape[0]

    weights2 = partner(weights, "replica", bit)
    upstream2 = partner(upstream, "dp", 0)
    here = lax.axis_index("dp")
    whole = lax.all_gather(tokens[0], "tensor", axis=1, tiled=True)
    mine = lax.dynamic_slice_in_dim(whole, here * rows, rows, 1)
    theirs = lax.dynamic_slice_in_dim(whole, (1 - here) * rows, rows, 1)
    mine2 = partner(theirs, "dp", 0)
    grad = contract(mine, upstream) + contract(mine2, upstream2)
    total = lax.psum(jnp.sum(grad * grad), ("dp", "tensor"))
    clip = jnp.minimum(1.0, 1.0 / jnp.sqrt(total / (D * FF) + 1e-06))
    first = (0.9 * first_moment.astype(jnp.float32) + 0.1 * (clip * grad)).astype(jnp.bfloat16)
    first2 = partner(first, "replica", bit)

    clip = clip.reshape(1, 1)
    arrived = [weights2, first2]
    start, chunks = 0, []
    for share in SHARES:
        size = rows * share // sum(SHARES)
        second = second_chunk(clip, grad, second_moment, arrived[-2], start, size)
        second2 = partner(second, "replica", bit)
        arrived.append(second2)
        chunks.append((start, second, second2))
        start += size
    outs = ()
    for start, second, second2 in chunks:
        outs = mix_chunk(weights, weights2, first, first2, second, second2, outs, start)
    return tuple(out[None] for out in outs)


def solution(mesh):
    placed = P("replica", "dp", "tensor")
    return jax.shard_map(
        body,
        mesh=mesh,
        in_specs=(placed,) * 5,
        out_specs=(placed,) * 3,
        check_vma=False,
    )
```

```python
import functools

import jax
import jax.numpy as jnp
from jax import lax
from jax.experimental import pallas as pl
from jax.experimental.pallas import tpu as pltpu
from jax.sharding import PartitionSpec as P

D = 2048
FF = 14336
STEP = 1
FIX_ONE = 1.0 - 0.9**STEP
FIX_TWO = 1.0 - 0.95**STEP
TILE = 32
BAND = 256
SHARES = (2, 4, 4, 4, 4, 4, 4, 3, 2, 1)


def partner(value, axis, bit):
    mask = 2**bit
    pairs = [(source, source ^ mask) for source in range(lax.axis_size(axis))]
    return lax.ppermute(value, axis, pairs)


def first_kernel(bit, tok, up, old, first_old, second_old, *refs):
    old2, first_out, first2 = refs[:3]
    chunks = refs[3 : 3 + len(SHARES)]
    (up_all, tok_all, turned, grad, first, second, square, squares) = refs[3 + len(SHARES) : -12]
    (old_send, old_recv, up_send, up_recv, hop_send, hop_recv, first_send, first_recv) = refs[-12:-4]
    fan_send, fan_recv, sum_send, sum_recv_local = refs[-4:]
    sum_recv, local = sum_recv_local.at[0], sum_recv_local.at[1]
    group, half, part = (lax.axis_index(name) for name in ("replica", "dp", "tensor"))
    parts = lax.axis_size("tensor")
    per = parts // 2
    count, feats = tok.shape
    rows, cols = old.shape
    partner_at = {"replica": group ^ 2**bit}
    other_at = {"dp": 1 - half}
    slot = lax.rem(part, per)
    owned = part // per == half

    def lines(which):
        return pl.ds(pl.multiple_of(which * count, count), count)

    def place(which, column):
        return tok_all.at[lines(which), pl.ds(pl.multiple_of(column * feats, feats), feats)]

    def remote(source, target, send, recv, where):
        return pltpu.make_async_remote_copy(
            src_ref=source,
            dst_ref=target,
            send_sem=send,
            recv_sem=recv,
            device_id=where,
            device_id_type=pl.DeviceIdType.MESH,
        )

    peers = [{"tensor": lax.rem(part + step, parts)} for step in range(1, parts)]
    across = [
        {"dp": 1 - half, "tensor": lax.rem(part + step, parts)} for step in range(parts)
    ]
    barrier = pltpu.get_barrier_semaphore()
    for where in [partner_at] + peers + across:
        pl.semaphore_signal(
            barrier, inc=1, device_id=where, device_id_type=pl.DeviceIdType.MESH
        )
    pl.semaphore_wait(barrier, 2 * parts)

    send_old = remote(old, old2, old_send, old_recv, partner_at)
    send_old.start()
    send_hop = remote(tok, place(half, slot), hop_send, hop_recv, other_at)
    came_hop = remote(tok, place(1 - half, slot), hop_send, hop_recv, other_at)

    def fan(step, kind):
        which = 1 - half if kind else half
        return remote(
            place(which, slot) if kind else tok,
            place(which, slot),
            fan_send.at[step, kind],
            fan_recv.at[slot, kind],
            peers[step],
        )

    keep_tok = pltpu.make_async_copy(tok, place(half, slot), local.at[0])

    @pl.when(jnp.logical_not(owned))
    def _():
        send_hop.start()

    @pl.when(owned)
    def _():
        for step in range(parts - 1):
            fan(step, 0).start()
        keep_tok.start()

    send_up = remote(up, up_all.at[lines(half)], up_send, up_recv, other_at)
    came_up = remote(up, up_all.at[lines(1 - half)], up_send, up_recv, other_at)
    send_up.start()
    keep_up = pltpu.make_async_copy(up, up_all.at[lines(half)], local.at[1])
    keep_up.start()
    load_first = pltpu.make_async_copy(first_old, first, local.at[2])
    load_first.start()
    load_second = pltpu.make_async_copy(second_old, second, local.at[3])
    load_second.start()

    @pl.when(jnp.logical_not(owned))
    def _():
        send_hop.wait_send()

    @pl.when(owned)
    def _():
        came_hop.wait_recv()
        for step in range(parts - 1):
            fan(step, 1).start()
        for step in range(parts - 1):
            fan(step, 0).wait_send()
            fan(step, 1).wait_send()
        keep_tok.wait()

    for index in range(per):

        @pl.when(part != half * per + index)
        def _(index=index):
            for kind, which in enumerate((half, 1 - half)):
                remote(
                    tok,
                    place(which, index),
                    fan_send.at[0, kind],
                    fan_recv.at[index, kind],
                    peers[0],
                ).wait_recv()

    turned[...] = tok_all[...].T
    square[...] = jnp.zeros_like(square)
    keep_up.wait()
    send_up.wait_send()
    came_up.wait_recv()
    bands = rows // BAND

    @pl.loop(0, bands * (cols // BAND))
    def _(index):
        high = pl.ds(pl.multiple_of(lax.rem(index, bands) * BAND, BAND), BAND)
        wide = pl.ds(pl.multiple_of(index // bands * BAND, BAND), BAND)
        product = jnp.dot(turned[high, :], up_all[:, wide], preferred_element_type=jnp.float32)
        grad[high, wide] = product
        square[...] += jnp.sum((product * product).reshape(BAND // 8, 8, BAND), axis=0)

    rank = half * parts + part
    sums = [
        remote(square, squares.at[rank], sum_send.at[index], sum_recv.at[rank], where)
        for index, where in enumerate(peers + across)
    ]
    for copy in sums:
        copy.start()
    squares[rank] = square[...]
    load_first.wait()
    load_second.wait()
    for copy in sums:
        copy.wait_send()
    for index in range(2 * parts):

        @pl.when(rank != index)
        def _(index=index):
            remote(
                square, squares.at[index], sum_send.at[0], sum_recv.at[index], peers[0]
            ).wait_recv()

    total = jnp.sum(squares[...], axis=0)
    total = jnp.sum(jnp.sum(total, axis=1, keepdims=True), axis=0, keepdims=True)
    clip = jnp.minimum(1.0, 1.0 / jnp.sqrt(total / (D * FF) + 1e-06))

    @pl.loop(0, rows // 16)
    def _(index):
        high = pl.ds(pl.multiple_of(index * 16, 16), 16)
        scaled = clip * grad[high, :]
        first[high, :] = (0.9 * first[high, :].astype(jnp.float32) + 0.1 * scaled).astype(
            jnp.bfloat16
        )

    send_first = remote(first, first2, first_send, first_recv, partner_at)
    send_first.start()
    keeps = [pltpu.make_async_copy(first, first_out, local.at[0])]
    keeps[0].start()

    @pl.loop(0, rows // 16)
    def _(index):
        high = pl.ds(pl.multiple_of(index * 16, 16), 16)
        scaled = clip * grad[high, :]
        second[high, :] = (
            0.95 * second[high, :].astype(jnp.float32) + 0.05 * scaled * scaled
        ).astype(jnp.bfloat16)

    start = 0
    for index, chunk in enumerate(chunks):
        size = chunk.shape[0]
        keep = pltpu.make_async_copy(second.at[pl.ds(start, size)], chunk, local.at[1 + index])
        keep.start()
        keeps.append(keep)
        start += size
    for keep in keeps:
        keep.wait()
    send_old.wait()
    send_first.wait()


def first_phase(tokens, upstream, weights, first_moment, second_moment, bit):
    count, feats = tokens.shape
    rows, cols = weights.shape
    parts = lax.axis_size("tensor")
    anywhere = pl.BlockSpec(memory_space=pl.ANY)
    dma = pltpu.SemaphoreType.DMA
    whole = jax.ShapeDtypeStruct((rows, cols), jnp.bfloat16)
    sizes = [rows * share // sum(SHARES) for share in SHARES]
    wide = max(2 * parts, 1 + len(SHARES), 4)
    outs = pl.pallas_call(
        functools.partial(first_kernel, bit),
        in_specs=[anywhere] * 5,
        out_specs=(anywhere,) * (3 + len(sizes)),
        out_shape=(whole,) * 3
        + tuple(jax.ShapeDtypeStruct((size, cols), jnp.bfloat16) for size in sizes),
        scratch_shapes=[
            pltpu.VMEM((2 * count, cols), jnp.bfloat16),
            pltpu.VMEM((2 * count, feats * (parts // 2)), jnp.bfloat16),
            pltpu.VMEM((feats * (parts // 2), 2 * count), jnp.bfloat16),
            pltpu.VMEM((rows, cols), jnp.float32),
            pltpu.VMEM((rows, cols), jnp.bfloat16),
            pltpu.VMEM((rows, cols), jnp.bfloat16),
            pltpu.VMEM((8, BAND), jnp.float32),
            pltpu.VMEM((2 * parts, 8, BAND), jnp.float32),
        ]
        + [dma(())] * 8
        + [dma((parts - 1, 2)), dma((parts // 2, 2)), dma((2 * parts - 1,)), dma((2, wide))],
        cost_estimate=pl.CostEstimate(
            flops=4 * count * rows * cols, bytes_accessed=20 * rows * cols, transcendentals=0
        ),
        compiler_params=pltpu.CompilerParams(
            collective_id=0, has_side_effects=True, vmem_limit_bytes=62 * 2**20
        ),
    )(tokens, upstream, weights, first_moment, second_moment)
    return outs[0], outs[1], outs[2], outs[3:]


def gate_kernel(value, *refs):
    refs[-1][...] = value[...]


def gate(value, after):
    rows, cols = value.shape
    block = pl.BlockSpec((TILE, cols), lambda i: (i, 0))
    return pl.pallas_call(
        gate_kernel,
        grid=(rows // TILE,),
        in_specs=[block] + [pl.BlockSpec(memory_space=pl.ANY)] * len(after),
        out_specs=block,
        out_shape=jax.ShapeDtypeStruct((rows, cols), jnp.bfloat16),
        cost_estimate=pl.CostEstimate(
            flops=0, bytes_accessed=4 * rows * cols, transcendentals=0
        ),
        compiler_params=pltpu.CompilerParams(vmem_limit_bytes=60 * 2**20),
    )(value, *after)


def new_weights(old, first, second):
    old = old.astype(jnp.float32)
    first = first.astype(jnp.float32)
    second = second.astype(jnp.float32)
    update = first / FIX_ONE / (jnp.sqrt(second / FIX_TWO) + 1e-08)
    fresh = old - 0.05 * (update + 0.1 * old)
    return fresh.astype(jnp.bfloat16)


def mean(one, two):
    return (0.5 * (one.astype(jnp.float32) + two.astype(jnp.float32))).astype(jnp.bfloat16)


def mix_kernel(w, w2, m, m2, v, v2, *refs):
    out_w, out_m, out_v, done = refs[-4:]
    first, first2 = m[...], m2[...]
    second, second2 = v[...], v2[...]
    out_m[...] = mean(first, first2)
    out_v[...] = mean(second, second2)
    out_w[...] = mean(
        new_weights(w[...], first, second), new_weights(w2[...], first2, second2)
    )
    done[...] = jnp.zeros_like(done)


def mix_chunk(w, w2, m, m2, v, v2, held, start):
    rows, cols = v.shape
    first = start // TILE
    far = pl.BlockSpec((TILE, cols), lambda i: (first + i, 0))
    near = pl.BlockSpec((TILE, cols), lambda i: (i, 0))
    *outs, done = pl.pallas_call(
        mix_kernel,
        grid=(rows // TILE,),
        in_specs=[far, far, far, far, near, near]
        + [pl.BlockSpec(memory_space=pl.ANY)] * len(held),
        out_specs=(far, far, far, pl.BlockSpec((8, 128), lambda i: (0, 0))),
        out_shape=(jax.ShapeDtypeStruct(w.shape, jnp.bfloat16),) * 3
        + (jax.ShapeDtypeStruct((8, 128), jnp.float32),),
        input_output_aliases={6 + i: i for i in range(len(held))},
        cost_estimate=pl.CostEstimate(
            flops=30 * rows * cols, bytes_accessed=18 * rows * cols, transcendentals=4 * rows * cols
        ),
        compiler_params=pltpu.CompilerParams(vmem_limit_bytes=60 * 2**20),
    )(w, w2, m, m2, v, v2, *held)
    return outs, done


def body(tokens, grad_out, weights, first_moment, second_moment):
    bit = lax.axis_size("replica").bit_length() - 2
    weights = weights[0]
    weights2, first, first2, chunks = first_phase(
        tokens[0], grad_out[0], weights, first_moment[0], second_moment[0], bit
    )
    arrived, mixed, outs, start = [], [], (), 0
    for index, second in enumerate(chunks):
        if index >= 2:
            after = [arrived[index - 2]]
            if index >= 3:
                after.append(mixed[index - 3])
            second = gate(second, after)
        second2 = partner(second, "replica", bit)
        arrived.append(second2)
        outs, done = mix_chunk(weights, weights2, first, first2, second, second2, outs, start)
        mixed.append(done)
        start += second.shape[0]
    return tuple(out[None] for out in outs)


def solution(mesh):
    placed = P("replica", "dp", "tensor")
    return jax.shard_map(
        body,
        mesh=mesh,
        in_specs=(placed,) * 5,
        out_specs=(placed,) * 3,
        check_vma=False,
    )
```

```python
import jax
import jax.numpy as jnp
from jax import lax
from jax.experimental import pallas as pl
from jax.experimental.pallas import tpu as pltpu
from jax.sharding import PartitionSpec as P

D = 2048
FF = 14336
STEP = 1
FIX_ONE = 1.0 - 0.9**STEP
FIX_TWO = 1.0 - 0.95**STEP
TILE = 32
BAND = 256
SHARES = (20, 4, 3, 3, 2)


def partner(value, axis, bit):
    mask = 2**bit
    pairs = [(source, source ^ mask) for source in range(lax.axis_size(axis))]
    return lax.ppermute(value, axis, pairs)


def first_kernel(tok, up, first_old, second_old, *refs):
    first_out, *chunks = refs[: 1 + len(SHARES)]
    (up_all, tok_all, turned, grad, first, second, square, squares) = refs[1 + len(SHARES) : -8]
    up_send, up_recv, hop_send, hop_recv = refs[-8:-4]
    fan_send, fan_recv, sum_send, sum_recv_local = refs[-4:]
    sum_recv, local = sum_recv_local.at[0], sum_recv_local.at[1]
    half, part = lax.axis_index("dp"), lax.axis_index("tensor")
    parts = lax.axis_size("tensor")
    per = parts // 2
    count, feats = tok.shape
    rows, cols = first_old.shape
    other_at = {"dp": 1 - half}
    slot = lax.rem(part, per)
    owned = part // per == half

    def lines(which):
        return pl.ds(pl.multiple_of(which * count, count), count)

    def place(which, column):
        return tok_all.at[lines(which), pl.ds(pl.multiple_of(column * feats, feats), feats)]

    def remote(source, target, send, recv, where):
        return pltpu.make_async_remote_copy(
            src_ref=source,
            dst_ref=target,
            send_sem=send,
            recv_sem=recv,
            device_id=where,
            device_id_type=pl.DeviceIdType.MESH,
        )

    peers = [{"tensor": lax.rem(part + step, parts)} for step in range(1, parts)]
    across = [
        {"dp": 1 - half, "tensor": lax.rem(part + step, parts)} for step in range(parts)
    ]
    barrier = pltpu.get_barrier_semaphore()
    for where in peers + across:
        pl.semaphore_signal(
            barrier, inc=1, device_id=where, device_id_type=pl.DeviceIdType.MESH
        )
    pl.semaphore_wait(barrier, 2 * parts - 1)

    send_hop = remote(tok, place(half, slot), hop_send, hop_recv, other_at)
    came_hop = remote(tok, place(1 - half, slot), hop_send, hop_recv, other_at)

    def fan(step, kind):
        which = 1 - half if kind else half
        return remote(
            place(which, slot) if kind else tok,
            place(which, slot),
            fan_send.at[step, kind],
            fan_recv.at[slot, kind],
            peers[step],
        )

    keep_tok = pltpu.make_async_copy(tok, place(half, slot), local.at[0])

    @pl.when(jnp.logical_not(owned))
    def _():
        send_hop.start()

    @pl.when(owned)
    def _():
        for step in range(parts - 1):
            fan(step, 0).start()
        keep_tok.start()

    send_up = remote(up, up_all.at[lines(half)], up_send, up_recv, other_at)
    came_up = remote(up, up_all.at[lines(1 - half)], up_send, up_recv, other_at)
    send_up.start()
    keep_up = pltpu.make_async_copy(up, up_all.at[lines(half)], local.at[1])
    keep_up.start()
    load_first = pltpu.make_async_copy(first_old, first, local.at[2])
    load_first.start()
    load_second = pltpu.make_async_copy(second_old, second, local.at[3])
    load_second.start()

    @pl.when(jnp.logical_not(owned))
    def _():
        send_hop.wait_send()

    @pl.when(owned)
    def _():
        came_hop.wait_recv()
        for step in range(parts - 1):
            fan(step, 1).start()
        for step in range(parts - 1):
            fan(step, 0).wait_send()
            fan(step, 1).wait_send()
        keep_tok.wait()

    for index in range(per):

        @pl.when(part != half * per + index)
        def _(index=index):
            for kind, which in enumerate((half, 1 - half)):
                remote(
                    tok,
                    place(which, index),
                    fan_send.at[0, kind],
                    fan_recv.at[index, kind],
                    peers[0],
                ).wait_recv()

    turned[...] = tok_all[...].T
    square[...] = jnp.zeros_like(square)
    keep_up.wait()
    send_up.wait_send()
    came_up.wait_recv()
    bands = rows // BAND

    @pl.loop(0, bands * (cols // BAND))
    def _(index):
        high = pl.ds(pl.multiple_of(lax.rem(index, bands) * BAND, BAND), BAND)
        wide = pl.ds(pl.multiple_of(index // bands * BAND, BAND), BAND)
        product = jnp.dot(turned[high, :], up_all[:, wide], preferred_element_type=jnp.float32)
        grad[high, wide] = product
        square[...] += jnp.sum((product * product).reshape(BAND // 8, 8, BAND), axis=0)

    rank = half * parts + part
    sums = [
        remote(square, squares.at[rank], sum_send.at[index], sum_recv.at[rank], where)
        for index, where in enumerate(peers + across)
    ]
    for copy in sums:
        copy.start()
    squares[rank] = square[...]
    load_first.wait()
    load_second.wait()
    for copy in sums:
        copy.wait_send()
    for index in range(2 * parts):

        @pl.when(rank != index)
        def _(index=index):
            remote(
                square, squares.at[index], sum_send.at[0], sum_recv.at[index], peers[0]
            ).wait_recv()

    total = jnp.sum(squares[...], axis=0)
    total = jnp.sum(jnp.sum(total, axis=1, keepdims=True), axis=0, keepdims=True)
    clip = jnp.minimum(1.0, 1.0 / jnp.sqrt(total / (D * FF) + 1e-06))

    @pl.loop(0, rows // 16)
    def _(index):
        high = pl.ds(pl.multiple_of(index * 16, 16), 16)
        scaled = clip * grad[high, :]
        first[high, :] = (0.9 * first[high, :].astype(jnp.float32) + 0.1 * scaled).astype(
            jnp.bfloat16
        )

    keeps = [pltpu.make_async_copy(first, first_out, local.at[0])]
    keeps[0].start()

    @pl.loop(0, rows // 16)
    def _(index):
        high = pl.ds(pl.multiple_of(index * 16, 16), 16)
        scaled = clip * grad[high, :]
        second[high, :] = (
            0.95 * second[high, :].astype(jnp.float32) + 0.05 * scaled * scaled
        ).astype(jnp.bfloat16)

    start = 0
    for index, chunk in enumerate(chunks):
        size = chunk.shape[0]
        keep = pltpu.make_async_copy(second.at[pl.ds(start, size)], chunk, local.at[1 + index])
        keep.start()
        keeps.append(keep)
        start += size
    for keep in keeps:
        keep.wait()


def first_phase(tokens, upstream, first_moment, second_moment):
    count, feats = tokens.shape
    rows, cols = first_moment.shape
    parts = lax.axis_size("tensor")
    anywhere = pl.BlockSpec(memory_space=pl.ANY)
    dma = pltpu.SemaphoreType.DMA
    whole = jax.ShapeDtypeStruct((rows, cols), jnp.bfloat16)
    sizes = [rows * share // sum(SHARES) for share in SHARES]
    wide = max(2 * parts, 1 + len(SHARES), 4)
    outs = pl.pallas_call(
        first_kernel,
        in_specs=[anywhere] * 4,
        out_specs=(anywhere,) * (1 + len(sizes)),
        out_shape=(whole,)
        + tuple(jax.ShapeDtypeStruct((size, cols), jnp.bfloat16) for size in sizes),
        scratch_shapes=[
            pltpu.VMEM((2 * count, cols), jnp.bfloat16),
            pltpu.VMEM((2 * count, feats * (parts // 2)), jnp.bfloat16),
            pltpu.VMEM((feats * (parts // 2), 2 * count), jnp.bfloat16),
            pltpu.VMEM((rows, cols), jnp.float32),
            pltpu.VMEM((rows, cols), jnp.bfloat16),
            pltpu.VMEM((rows, cols), jnp.bfloat16),
            pltpu.VMEM((8, BAND), jnp.float32),
            pltpu.VMEM((2 * parts, 8, BAND), jnp.float32),
        ]
        + [dma(())] * 4
        + [dma((parts - 1, 2)), dma((parts // 2, 2)), dma((2 * parts - 1,)), dma((2, wide))],
        cost_estimate=pl.CostEstimate(
            flops=4 * count * rows * cols, bytes_accessed=20 * rows * cols, transcendentals=0
        ),
        compiler_params=pltpu.CompilerParams(
            collective_id=0, has_side_effects=True, vmem_limit_bytes=62 * 2**20
        ),
    )(tokens, upstream, first_moment, second_moment)
    return outs[0], outs[1:]


def gate_kernel(value, *refs):
    refs[-1][...] = value[...]


def gate(value, after):
    rows, cols = value.shape
    block = pl.BlockSpec((TILE, cols), lambda i: (i, 0))
    return pl.pallas_call(
        gate_kernel,
        grid=(rows // TILE,),
        in_specs=[block] + [pl.BlockSpec(memory_space=pl.ANY)] * len(after),
        out_specs=block,
        out_shape=jax.ShapeDtypeStruct((rows, cols), jnp.bfloat16),
        cost_estimate=pl.CostEstimate(
            flops=0, bytes_accessed=4 * rows * cols, transcendentals=0
        ),
        compiler_params=pltpu.CompilerParams(vmem_limit_bytes=60 * 2**20),
    )(value, *after)


def new_weights(old, first, second):
    old = old.astype(jnp.float32)
    first = first.astype(jnp.float32)
    second = second.astype(jnp.float32)
    update = first / FIX_ONE / (jnp.sqrt(second / FIX_TWO) + 1e-08)
    fresh = old - 0.05 * (update + 0.1 * old)
    return fresh.astype(jnp.bfloat16)


def mean(one, two):
    return (0.5 * (one.astype(jnp.float32) + two.astype(jnp.float32))).astype(jnp.bfloat16)


def mix_kernel(w, w2, m, m2, v, v2, *refs):
    out_w, out_m, out_v, done = refs[-4:]
    first, first2 = m[...], m2[...]
    second, second2 = v[...], v2[...]
    out_m[...] = mean(first, first2)
    out_v[...] = mean(second, second2)
    out_w[...] = mean(
        new_weights(w[...], first, second), new_weights(w2[...], first2, second2)
    )
    done[...] = jnp.zeros_like(done)


def mix_chunk(w, w2, m, m2, v, v2, held, start):
    rows, cols = v.shape
    first = start // TILE
    far = pl.BlockSpec((TILE, cols), lambda i: (first + i, 0))
    near = pl.BlockSpec((TILE, cols), lambda i: (i, 0))
    *outs, done = pl.pallas_call(
        mix_kernel,
        grid=(rows // TILE,),
        in_specs=[far, far, far, far, near, near]
        + [pl.BlockSpec(memory_space=pl.ANY)] * len(held),
        out_specs=(far, far, far, pl.BlockSpec((8, 128), lambda i: (0, 0))),
        out_shape=(jax.ShapeDtypeStruct(w.shape, jnp.bfloat16),) * 3
        + (jax.ShapeDtypeStruct((8, 128), jnp.float32),),
        input_output_aliases={6 + i: i for i in range(len(held))},
        cost_estimate=pl.CostEstimate(
            flops=30 * rows * cols, bytes_accessed=18 * rows * cols, transcendentals=4 * rows * cols
        ),
        compiler_params=pltpu.CompilerParams(vmem_limit_bytes=60 * 2**20),
    )(w, w2, m, m2, v, v2, *held)
    return outs, done


def body(tokens, grad_out, weights, first_moment, second_moment):
    bit = lax.axis_size("replica").bit_length() - 2
    weights = weights[0]
    weights2 = partner(weights, "replica", bit)
    first, chunks = first_phase(tokens[0], grad_out[0], first_moment[0], second_moment[0])
    first2 = partner(first, "replica", bit)
    arrived, mixed, outs, start = [], [], (), 0
    waits = (weights2, 0, first2, 1, 2)
    for index, second in enumerate(chunks):
        wait = waits[index]
        after = [arrived[wait] if isinstance(wait, int) else wait]
        if index >= 3:
            after.append(mixed[index - 3])
        second = gate(second, after)
        second2 = partner(second, "replica", bit)
        arrived.append(second2)
        outs, done = mix_chunk(weights, weights2, first, first2, second, second2, outs, start)
        mixed.append(done)
        start += second.shape[0]
    return tuple(out[None] for out in outs)


def solution(mesh):
    placed = P("replica", "dp", "tensor")
    return jax.shard_map(
        body,
        mesh=mesh,
        in_specs=(placed,) * 5,
        out_specs=(placed,) * 3,
        check_vma=False,
    )
```

```python
import jax
import jax.numpy as jnp
from jax import lax
from jax.experimental import pallas as pl
from jax.experimental.pallas import tpu as pltpu
from jax.sharding import PartitionSpec as P

D = 2048
FF = 14336
STEP = 1
FIX_ONE = 1.0 - 0.9**STEP
FIX_TWO = 1.0 - 0.95**STEP
TILE = 32
BAND = 256
SHARES = (20, 4, 3, 3, 2)


def partner(value, axis, bit):
    mask = 2**bit
    pairs = [(source, source ^ mask) for source in range(lax.axis_size(axis))]
    return lax.ppermute(value, axis, pairs)


def back(value, axis):
    size = lax.axis_size(axis)
    step = size // 4
    pairs = [(source, (source - step) % size) for source in range(size)]
    return lax.ppermute(value, axis, pairs)


def first_kernel(tok, up, first_old, second_old, *refs):
    first_out, *chunks = refs[: 1 + len(SHARES)]
    (up_all, tok_all, turned, grad, first, second, square, squares) = refs[1 + len(SHARES) : -8]
    up_send, up_recv, hop_send, hop_recv = refs[-8:-4]
    fan_send, fan_recv, sum_send, sum_recv_local = refs[-4:]
    sum_recv, local = sum_recv_local.at[0], sum_recv_local.at[1]
    half, part = lax.axis_index("dp"), lax.axis_index("tensor")
    parts = lax.axis_size("tensor")
    per = parts // 2
    count, feats = tok.shape
    rows, cols = first_old.shape
    other_at = {"dp": 1 - half}
    slot = lax.rem(part, per)
    owned = part // per == half

    def lines(which):
        return pl.ds(pl.multiple_of(which * count, count), count)

    def place(which, column):
        return tok_all.at[lines(which), pl.ds(pl.multiple_of(column * feats, feats), feats)]

    def remote(source, target, send, recv, where):
        return pltpu.make_async_remote_copy(
            src_ref=source,
            dst_ref=target,
            send_sem=send,
            recv_sem=recv,
            device_id=where,
            device_id_type=pl.DeviceIdType.MESH,
        )

    peers = [{"tensor": lax.rem(part + step, parts)} for step in range(1, parts)]
    across = [
        {"dp": 1 - half, "tensor": lax.rem(part + step, parts)} for step in range(parts)
    ]
    barrier = pltpu.get_barrier_semaphore()
    for where in peers + across:
        pl.semaphore_signal(
            barrier, inc=1, device_id=where, device_id_type=pl.DeviceIdType.MESH
        )
    pl.semaphore_wait(barrier, 2 * parts - 1)

    send_hop = remote(tok, place(half, slot), hop_send, hop_recv, other_at)
    came_hop = remote(tok, place(1 - half, slot), hop_send, hop_recv, other_at)

    def fan(step, kind):
        which = 1 - half if kind else half
        return remote(
            place(which, slot) if kind else tok,
            place(which, slot),
            fan_send.at[step, kind],
            fan_recv.at[slot, kind],
            peers[step],
        )

    keep_tok = pltpu.make_async_copy(tok, place(half, slot), local.at[0])

    @pl.when(jnp.logical_not(owned))
    def _():
        send_hop.start()

    @pl.when(owned)
    def _():
        for step in range(parts - 1):
            fan(step, 0).start()
        keep_tok.start()

    send_up = remote(up, up_all.at[lines(half)], up_send, up_recv, other_at)
    came_up = remote(up, up_all.at[lines(1 - half)], up_send, up_recv, other_at)
    send_up.start()
    keep_up = pltpu.make_async_copy(up, up_all.at[lines(half)], local.at[1])
    keep_up.start()
    load_first = pltpu.make_async_copy(first_old, first, local.at[2])
    load_first.start()
    load_second = pltpu.make_async_copy(second_old, second, local.at[3])
    load_second.start()

    @pl.when(jnp.logical_not(owned))
    def _():
        send_hop.wait_send()

    @pl.when(owned)
    def _():
        came_hop.wait_recv()
        for step in range(parts - 1):
            fan(step, 1).start()
        for step in range(parts - 1):
            fan(step, 0).wait_send()
            fan(step, 1).wait_send()
        keep_tok.wait()

    for index in range(per):

        @pl.when(part != half * per + index)
        def _(index=index):
            for kind, which in enumerate((half, 1 - half)):
                remote(
                    tok,
                    place(which, index),
                    fan_send.at[0, kind],
                    fan_recv.at[index, kind],
                    peers[0],
                ).wait_recv()

    turned[...] = tok_all[...].T
    square[...] = jnp.zeros_like(square)
    keep_up.wait()
    send_up.wait_send()
    came_up.wait_recv()
    bands = rows // BAND

    @pl.loop(0, bands * (cols // BAND))
    def _(index):
        high = pl.ds(pl.multiple_of(lax.rem(index, bands) * BAND, BAND), BAND)
        wide = pl.ds(pl.multiple_of(index // bands * BAND, BAND), BAND)
        product = jnp.dot(turned[high, :], up_all[:, wide], preferred_element_type=jnp.float32)
        grad[high, wide] = product
        square[...] += jnp.sum((product * product).reshape(BAND // 8, 8, BAND), axis=0)

    rank = half * parts + part
    sums = [
        remote(square, squares.at[rank], sum_send.at[index], sum_recv.at[rank], where)
        for index, where in enumerate(peers + across)
    ]
    for copy in sums:
        copy.start()
    squares[rank] = square[...]
    load_first.wait()
    load_second.wait()
    for copy in sums:
        copy.wait_send()
    for index in range(2 * parts):

        @pl.when(rank != index)
        def _(index=index):
            remote(
                square, squares.at[index], sum_send.at[0], sum_recv.at[index], peers[0]
            ).wait_recv()

    total = jnp.sum(squares[...], axis=0)
    total = jnp.sum(jnp.sum(total, axis=1, keepdims=True), axis=0, keepdims=True)
    clip = jnp.minimum(1.0, 1.0 / jnp.sqrt(total / (D * FF) + 1e-06))

    @pl.loop(0, rows // 16)
    def _(index):
        high = pl.ds(pl.multiple_of(index * 16, 16), 16)
        scaled = clip * grad[high, :]
        first[high, :] = (0.9 * first[high, :].astype(jnp.float32) + 0.1 * scaled).astype(
            jnp.bfloat16
        )

    keeps = [pltpu.make_async_copy(first, first_out, local.at[0])]
    keeps[0].start()

    @pl.loop(0, rows // 16)
    def _(index):
        high = pl.ds(pl.multiple_of(index * 16, 16), 16)
        scaled = clip * grad[high, :]
        second[high, :] = (
            0.95 * second[high, :].astype(jnp.float32) + 0.05 * scaled * scaled
        ).astype(jnp.bfloat16)

    start = 0
    for index, chunk in enumerate(chunks):
        size = chunk.shape[0]
        keep = pltpu.make_async_copy(second.at[pl.ds(start, size)], chunk, local.at[1 + index])
        keep.start()
        keeps.append(keep)
        start += size
    for keep in keeps:
        keep.wait()


def first_phase(tokens, upstream, first_moment, second_moment):
    count, feats = tokens.shape
    rows, cols = first_moment.shape
    parts = lax.axis_size("tensor")
    anywhere = pl.BlockSpec(memory_space=pl.ANY)
    dma = pltpu.SemaphoreType.DMA
    whole = jax.ShapeDtypeStruct((rows, cols), jnp.bfloat16)
    sizes = [rows * share // sum(SHARES) for share in SHARES]
    wide = max(2 * parts, 1 + len(SHARES), 4)
    outs = pl.pallas_call(
        first_kernel,
        in_specs=[anywhere] * 4,
        out_specs=(anywhere,) * (1 + len(sizes)),
        out_shape=(whole,)
        + tuple(jax.ShapeDtypeStruct((size, cols), jnp.bfloat16) for size in sizes),
        scratch_shapes=[
            pltpu.VMEM((2 * count, cols), jnp.bfloat16),
            pltpu.VMEM((2 * count, feats * (parts // 2)), jnp.bfloat16),
            pltpu.VMEM((feats * (parts // 2), 2 * count), jnp.bfloat16),
            pltpu.VMEM((rows, cols), jnp.float32),
            pltpu.VMEM((rows, cols), jnp.bfloat16),
            pltpu.VMEM((rows, cols), jnp.bfloat16),
            pltpu.VMEM((8, BAND), jnp.float32),
            pltpu.VMEM((2 * parts, 8, BAND), jnp.float32),
        ]
        + [dma(())] * 4
        + [dma((parts - 1, 2)), dma((parts // 2, 2)), dma((2 * parts - 1,)), dma((2, wide))],
        cost_estimate=pl.CostEstimate(
            flops=4 * count * rows * cols, bytes_accessed=20 * rows * cols, transcendentals=0
        ),
        compiler_params=pltpu.CompilerParams(
            collective_id=0, has_side_effects=True, vmem_limit_bytes=62 * 2**20
        ),
    )(tokens, upstream, first_moment, second_moment)
    return outs[0], outs[1:]


def gate_kernel(value, *refs):
    refs[-1][...] = value[...]


def gate(value, after):
    rows, cols = value.shape
    block = pl.BlockSpec((TILE, cols), lambda i: (i, 0))
    return pl.pallas_call(
        gate_kernel,
        grid=(rows // TILE,),
        in_specs=[block] + [pl.BlockSpec(memory_space=pl.ANY)] * len(after),
        out_specs=block,
        out_shape=jax.ShapeDtypeStruct((rows, cols), jnp.bfloat16),
        cost_estimate=pl.CostEstimate(
            flops=0, bytes_accessed=4 * rows * cols, transcendentals=0
        ),
        compiler_params=pltpu.CompilerParams(vmem_limit_bytes=60 * 2**20),
    )(value, *after)


def new_weights(old, first, second):
    old = old.astype(jnp.float32)
    first = first.astype(jnp.float32)
    second = second.astype(jnp.float32)
    update = first / FIX_ONE / (jnp.sqrt(second / FIX_TWO) + 1e-08)
    fresh = old - 0.05 * (update + 0.1 * old)
    return fresh.astype(jnp.bfloat16)


def mean(one, two):
    return (0.5 * (one.astype(jnp.float32) + two.astype(jnp.float32))).astype(jnp.bfloat16)


def mix_kernel(w, w2, m, m2, v, v2, *refs):
    out_w, out_m, out_v, done = refs[-4:]
    first, first2 = m[...], m2[...]
    second, second2 = v[...], v2[...]
    out_m[...] = mean(first, first2)
    out_v[...] = mean(second, second2)
    out_w[...] = mean(
        new_weights(w[...], first, second), new_weights(w2[...], first2, second2)
    )
    done[...] = jnp.zeros_like(done)


def mix_chunk(w, w2, m, m2, v, v2, held, start):
    rows, cols = v.shape
    first = start // TILE
    far = pl.BlockSpec((TILE, cols), lambda i: (first + i, 0))
    near = pl.BlockSpec((TILE, cols), lambda i: (i, 0))
    *outs, done = pl.pallas_call(
        mix_kernel,
        grid=(rows // TILE,),
        in_specs=[far, far, far, far, near, near]
        + [pl.BlockSpec(memory_space=pl.ANY)] * len(held),
        out_specs=(far, far, far, pl.BlockSpec((8, 128), lambda i: (0, 0))),
        out_shape=(jax.ShapeDtypeStruct(w.shape, jnp.bfloat16),) * 3
        + (jax.ShapeDtypeStruct((8, 128), jnp.float32),),
        input_output_aliases={6 + i: i for i in range(len(held))},
        cost_estimate=pl.CostEstimate(
            flops=30 * rows * cols, bytes_accessed=18 * rows * cols, transcendentals=4 * rows * cols
        ),
        compiler_params=pltpu.CompilerParams(vmem_limit_bytes=60 * 2**20),
    )(w, w2, m, m2, v, v2, *held)
    return outs, done


def body(tokens, grad_out, weights, first_moment, second_moment):
    bit = lax.axis_size("replica").bit_length() - 2
    weights = weights[0]
    weights2 = partner(weights, "replica", bit)
    first, chunks = first_phase(tokens[0], grad_out[0], first_moment[0], second_moment[0])
    first2 = partner(first, "replica", bit)
    arrived, mixed, outs, start = [], [], (), 0
    waits = (weights2, 0, first2, 1, 2)
    for index, second in enumerate(chunks):
        wait = waits[index]
        after = [arrived[wait] if isinstance(wait, int) else wait]
        if index >= 3:
            after.append(mixed[index - 3])
        if index:
            second = gate(second, after)
            second2 = partner(second, "replica", bit)
        else:
            second2 = back(back(second, "replica"), "replica")
        arrived.append(second2)
        outs, done = mix_chunk(weights, weights2, first, first2, second, second2, outs, start)
        mixed.append(done)
        start += second.shape[0]
    return tuple(out[None] for out in outs)


def solution(mesh):
    placed = P("replica", "dp", "tensor")
    return jax.shard_map(
        body,
        mesh=mesh,
        in_specs=(placed,) * 5,
        out_specs=(placed,) * 3,
        check_vma=False,
    )
```

```python
import functools

import jax
import jax.numpy as jnp
from jax import lax
from jax.experimental import pallas as pl
from jax.experimental.pallas import tpu as pltpu
from jax.sharding import PartitionSpec as P

D = 2048
FF = 14336
STEP = 1
FIX_ONE = 1.0 - 0.9**STEP
FIX_TWO = 1.0 - 0.95**STEP
TILE = 32
BAND = 256
PIECES = 4
SHARES = (2, 4, 4, 4, 4, 4, 4, 3, 2, 1)


def partner(value, axis, bit):
    mask = 2**bit
    pairs = [(source, source ^ mask) for source in range(lax.axis_size(axis))]
    return lax.ppermute(value, axis, pairs)


def first_kernel(bit, tok, up, old, first_old, second_old, *refs):
    old2, first_out, first2 = refs[:3]
    chunks = refs[3 : 3 + len(SHARES)]
    (up_all, tok_all, turned, grad, first, second, square, squares) = refs[3 + len(SHARES) : -12]
    (old_send, old_recv, up_send, up_recv, hop_send, hop_recv, first_send, first_recv) = refs[-12:-4]
    fan_send, fan_recv, sum_send, sum_recv_local = refs[-4:]
    sum_recv, local = sum_recv_local.at[0], sum_recv_local.at[1]
    group, half, part = (lax.axis_index(name) for name in ("replica", "dp", "tensor"))
    parts = lax.axis_size("tensor")
    per = parts // 2
    count, feats = tok.shape
    rows, cols = old.shape
    partner_at = {"replica": group ^ 2**bit}
    other_at = {"dp": 1 - half}
    slot = lax.rem(part, per)
    owned = part // per == half

    def lines(which):
        return pl.ds(pl.multiple_of(which * count, count), count)

    def place(which, column):
        return tok_all.at[lines(which), pl.ds(pl.multiple_of(column * feats, feats), feats)]

    def remote(source, target, send, recv, where):
        return pltpu.make_async_remote_copy(
            src_ref=source,
            dst_ref=target,
            send_sem=send,
            recv_sem=recv,
            device_id=where,
            device_id_type=pl.DeviceIdType.MESH,
        )

    peers = [{"tensor": lax.rem(part + step, parts)} for step in range(1, parts)]
    across = [
        {"dp": 1 - half, "tensor": lax.rem(part + step, parts)} for step in range(parts)
    ]
    barrier = pltpu.get_barrier_semaphore()
    for where in [partner_at] + peers + across:
        pl.semaphore_signal(
            barrier, inc=1, device_id=where, device_id_type=pl.DeviceIdType.MESH
        )
    pl.semaphore_wait(barrier, 2 * parts)

    size = rows // PIECES
    pieces = [pl.ds(index * size, size) for index in range(PIECES)]
    send_old = [
        remote(old.at[piece], old2.at[piece], old_send.at[index], old_recv.at[index], partner_at)
        for index, piece in enumerate(pieces)
    ]
    for copy in send_old:
        copy.start()
    send_hop = remote(tok, place(half, slot), hop_send, hop_recv, other_at)
    came_hop = remote(tok, place(1 - half, slot), hop_send, hop_recv, other_at)

    def fan(step, kind):
        which = 1 - half if kind else half
        return remote(
            place(which, slot) if kind else tok,
            place(which, slot),
            fan_send.at[step, kind],
            fan_recv.at[slot, kind],
            peers[step],
        )

    keep_tok = pltpu.make_async_copy(tok, place(half, slot), local.at[0])

    @pl.when(jnp.logical_not(owned))
    def _():
        send_hop.start()

    @pl.when(owned)
    def _():
        for step in range(parts - 1):
            fan(step, 0).start()
        keep_tok.start()

    send_up = remote(up, up_all.at[lines(half)], up_send, up_recv, other_at)
    came_up = remote(up, up_all.at[lines(1 - half)], up_send, up_recv, other_at)
    send_up.start()
    keep_up = pltpu.make_async_copy(up, up_all.at[lines(half)], local.at[1])
    keep_up.start()
    load_first = pltpu.make_async_copy(first_old, first, local.at[2])
    load_first.start()
    load_second = pltpu.make_async_copy(second_old, second, local.at[3])
    load_second.start()

    @pl.when(jnp.logical_not(owned))
    def _():
        send_hop.wait_send()

    @pl.when(owned)
    def _():
        came_hop.wait_recv()
        for step in range(parts - 1):
            fan(step, 1).start()
        for step in range(parts - 1):
            fan(step, 0).wait_send()
            fan(step, 1).wait_send()
        keep_tok.wait()

    for index in range(per):

        @pl.when(part != half * per + index)
        def _(index=index):
            for kind, which in enumerate((half, 1 - half)):
                remote(
                    tok,
                    place(which, index),
                    fan_send.at[0, kind],
                    fan_recv.at[index, kind],
                    peers[0],
                ).wait_recv()

    turned[...] = tok_all[...].T
    square[...] = jnp.zeros_like(square)
    keep_up.wait()
    send_up.wait_send()
    came_up.wait_recv()
    bands = rows // BAND

    @pl.loop(0, bands * (cols // BAND))
    def _(index):
        high = pl.ds(pl.multiple_of(lax.rem(index, bands) * BAND, BAND), BAND)
        wide = pl.ds(pl.multiple_of(index // bands * BAND, BAND), BAND)
        product = jnp.dot(turned[high, :], up_all[:, wide], preferred_element_type=jnp.float32)
        grad[high, wide] = product
        square[...] += jnp.sum((product * product).reshape(BAND // 8, 8, BAND), axis=0)

    rank = half * parts + part
    sums = [
        remote(square, squares.at[rank], sum_send.at[index], sum_recv.at[rank], where)
        for index, where in enumerate(peers + across)
    ]
    for copy in sums:
        copy.start()
    squares[rank] = square[...]
    load_first.wait()
    load_second.wait()
    for copy in sums:
        copy.wait_send()
    for index in range(2 * parts):

        @pl.when(rank != index)
        def _(index=index):
            remote(
                square, squares.at[index], sum_send.at[0], sum_recv.at[index], peers[0]
            ).wait_recv()

    total = jnp.sum(squares[...], axis=0)
    total = jnp.sum(jnp.sum(total, axis=1, keepdims=True), axis=0, keepdims=True)
    clip = jnp.minimum(1.0, 1.0 / jnp.sqrt(total / (D * FF) + 1e-06))

    send_first = []
    for index, piece in enumerate(pieces):

        @pl.loop(index * size // 16, (index + 1) * size // 16)
        def _(step):
            high = pl.ds(pl.multiple_of(step * 16, 16), 16)
            scaled = clip * grad[high, :]
            first[high, :] = (0.9 * first[high, :].astype(jnp.float32) + 0.1 * scaled).astype(
                jnp.bfloat16
            )

        copy = remote(
            first.at[piece], first2.at[piece], first_send.at[index], first_recv.at[index], partner_at
        )
        copy.start()
        send_first.append(copy)

    keeps = [pltpu.make_async_copy(first, first_out, local.at[0])]
    keeps[0].start()

    @pl.loop(0, rows // 16)
    def _(index):
        high = pl.ds(pl.multiple_of(index * 16, 16), 16)
        scaled = clip * grad[high, :]
        second[high, :] = (
            0.95 * second[high, :].astype(jnp.float32) + 0.05 * scaled * scaled
        ).astype(jnp.bfloat16)

    start = 0
    for index, chunk in enumerate(chunks):
        size = chunk.shape[0]
        keep = pltpu.make_async_copy(second.at[pl.ds(start, size)], chunk, local.at[1 + index])
        keep.start()
        keeps.append(keep)
        start += size
    for keep in keeps:
        keep.wait()
    for copy in send_old + send_first:
        copy.wait()


def first_phase(tokens, upstream, weights, first_moment, second_moment, bit):
    count, feats = tokens.shape
    rows, cols = weights.shape
    parts = lax.axis_size("tensor")
    anywhere = pl.BlockSpec(memory_space=pl.ANY)
    dma = pltpu.SemaphoreType.DMA
    whole = jax.ShapeDtypeStruct((rows, cols), jnp.bfloat16)
    sizes = [rows * share // sum(SHARES) for share in SHARES]
    wide = max(2 * parts, 1 + len(SHARES), 4)
    outs = pl.pallas_call(
        functools.partial(first_kernel, bit),
        in_specs=[anywhere] * 5,
        out_specs=(anywhere,) * (3 + len(sizes)),
        out_shape=(whole,) * 3
        + tuple(jax.ShapeDtypeStruct((size, cols), jnp.bfloat16) for size in sizes),
        scratch_shapes=[
            pltpu.VMEM((2 * count, cols), jnp.bfloat16),
            pltpu.VMEM((2 * count, feats * (parts // 2)), jnp.bfloat16),
            pltpu.VMEM((feats * (parts // 2), 2 * count), jnp.bfloat16),
            pltpu.VMEM((rows, cols), jnp.float32),
            pltpu.VMEM((rows, cols), jnp.bfloat16),
            pltpu.VMEM((rows, cols), jnp.bfloat16),
            pltpu.VMEM((8, BAND), jnp.float32),
            pltpu.VMEM((2 * parts, 8, BAND), jnp.float32),
        ]
        + [dma((PIECES,))] * 2
        + [dma(())] * 4
        + [dma((PIECES,))] * 2
        + [dma((parts - 1, 2)), dma((parts // 2, 2)), dma((2 * parts - 1,)), dma((2, wide))],
        cost_estimate=pl.CostEstimate(
            flops=4 * count * rows * cols, bytes_accessed=20 * rows * cols, transcendentals=0
        ),
        compiler_params=pltpu.CompilerParams(
            collective_id=0, has_side_effects=True, vmem_limit_bytes=62 * 2**20
        ),
    )(tokens, upstream, weights, first_moment, second_moment)
    return outs[0], outs[1], outs[2], outs[3:]


def gate_kernel(value, *refs):
    refs[-1][...] = value[...]


def gate(value, after):
    rows, cols = value.shape
    block = pl.BlockSpec((TILE, cols), lambda i: (i, 0))
    return pl.pallas_call(
        gate_kernel,
        grid=(rows // TILE,),
        in_specs=[block] + [pl.BlockSpec(memory_space=pl.ANY)] * len(after),
        out_specs=block,
        out_shape=jax.ShapeDtypeStruct((rows, cols), jnp.bfloat16),
        cost_estimate=pl.CostEstimate(
            flops=0, bytes_accessed=4 * rows * cols, transcendentals=0
        ),
        compiler_params=pltpu.CompilerParams(vmem_limit_bytes=60 * 2**20),
    )(value, *after)


def new_weights(old, first, second):
    old = old.astype(jnp.float32)
    first = first.astype(jnp.float32)
    second = second.astype(jnp.float32)
    update = first * (1.0 / FIX_ONE) / (jnp.sqrt(second * (1.0 / FIX_TWO)) + 1e-08)
    fresh = old - 0.05 * (update + 0.1 * old)
    return fresh.astype(jnp.bfloat16)


def mean(one, two):
    return (0.5 * (one.astype(jnp.float32) + two.astype(jnp.float32))).astype(jnp.bfloat16)


def mix_kernel(w, w2, m, m2, v, v2, *refs):
    out_w, out_m, out_v, done = refs[-4:]
    first, first2 = m[...], m2[...]
    second, second2 = v[...], v2[...]
    out_m[...] = mean(first, first2)
    out_v[...] = mean(second, second2)
    out_w[...] = mean(
        new_weights(w[...], first, second), new_weights(w2[...], first2, second2)
    )
    done[...] = jnp.zeros_like(done)


def mix_chunk(w, w2, m, m2, v, v2, held, start):
    rows, cols = v.shape
    first = start // TILE
    far = pl.BlockSpec((TILE, cols), lambda i: (first + i, 0))
    near = pl.BlockSpec((TILE, cols), lambda i: (i, 0))
    *outs, done = pl.pallas_call(
        mix_kernel,
        grid=(rows // TILE,),
        in_specs=[far, far, far, far, near, near]
        + [pl.BlockSpec(memory_space=pl.ANY)] * len(held),
        out_specs=(far, far, far, pl.BlockSpec((8, 128), lambda i: (0, 0))),
        out_shape=(jax.ShapeDtypeStruct(w.shape, jnp.bfloat16),) * 3
        + (jax.ShapeDtypeStruct((8, 128), jnp.float32),),
        input_output_aliases={6 + i: i for i in range(len(held))},
        cost_estimate=pl.CostEstimate(
            flops=30 * rows * cols, bytes_accessed=18 * rows * cols, transcendentals=4 * rows * cols
        ),
        compiler_params=pltpu.CompilerParams(vmem_limit_bytes=60 * 2**20),
    )(w, w2, m, m2, v, v2, *held)
    return outs, done


def body(tokens, grad_out, weights, first_moment, second_moment):
    bit = lax.axis_size("replica").bit_length() - 2
    weights = weights[0]
    weights2, first, first2, chunks = first_phase(
        tokens[0], grad_out[0], weights, first_moment[0], second_moment[0], bit
    )
    arrived, mixed, outs, start = [], [], (), 0
    for index, second in enumerate(chunks):
        if index >= 2:
            after = [arrived[index - 2]]
            if index >= 3:
                after.append(mixed[index - 3])
            second = gate(second, after)
        second2 = partner(second, "replica", bit)
        arrived.append(second2)
        outs, done = mix_chunk(weights, weights2, first, first2, second, second2, outs, start)
        mixed.append(done)
        start += second.shape[0]
    return tuple(out[None] for out in outs)


def solution(mesh):
    placed = P("replica", "dp", "tensor")
    return jax.shard_map(
        body,
        mesh=mesh,
        in_specs=(placed,) * 5,
        out_specs=(placed,) * 3,
        check_vma=False,
    )
```

```python
import jax
import jax.numpy as jnp
from jax import lax
from jax.experimental import pallas as pl
from jax.experimental.pallas import tpu as pltpu
from jax.sharding import PartitionSpec as P

D = 2048
FF = 14336
STEP = 1
FIX_ONE = 1.0 - 0.9**STEP
FIX_TWO = 1.0 - 0.95**STEP
TILE = 32
BAND = 256
SHARES = (12, 5, 4, 4, 3, 2, 2)


def partner(value, axis, bit):
    mask = 2**bit
    pairs = [(source, source ^ mask) for source in range(lax.axis_size(axis))]
    return lax.ppermute(value, axis, pairs)


def first_kernel(tok, up, first_old, second_old, *refs):
    first_out, *chunks = refs[: 1 + len(SHARES)]
    (up_all, tok_all, turned, grad, first, second, square, squares) = refs[1 + len(SHARES) : -8]
    up_send, up_recv, hop_send, hop_recv = refs[-8:-4]
    fan_send, fan_recv, sum_send, sum_recv_local = refs[-4:]
    sum_recv, local = sum_recv_local.at[0], sum_recv_local.at[1]
    half, part = lax.axis_index("dp"), lax.axis_index("tensor")
    parts = lax.axis_size("tensor")
    per = parts // 2
    count, feats = tok.shape
    rows, cols = first_old.shape
    other_at = {"dp": 1 - half}
    slot = lax.rem(part, per)
    owned = part // per == half

    def lines(which):
        return pl.ds(pl.multiple_of(which * count, count), count)

    def place(which, column):
        return tok_all.at[lines(which), pl.ds(pl.multiple_of(column * feats, feats), feats)]

    def remote(source, target, send, recv, where):
        return pltpu.make_async_remote_copy(
            src_ref=source,
            dst_ref=target,
            send_sem=send,
            recv_sem=recv,
            device_id=where,
            device_id_type=pl.DeviceIdType.MESH,
        )

    peers = [{"tensor": lax.rem(part + step, parts)} for step in range(1, parts)]
    across = [
        {"dp": 1 - half, "tensor": lax.rem(part + step, parts)} for step in range(parts)
    ]
    barrier = pltpu.get_barrier_semaphore()
    for where in peers + across:
        pl.semaphore_signal(
            barrier, inc=1, device_id=where, device_id_type=pl.DeviceIdType.MESH
        )
    pl.semaphore_wait(barrier, 2 * parts - 1)

    send_hop = remote(tok, place(half, slot), hop_send, hop_recv, other_at)
    came_hop = remote(tok, place(1 - half, slot), hop_send, hop_recv, other_at)

    def fan(step, kind):
        which = 1 - half if kind else half
        return remote(
            place(which, slot) if kind else tok,
            place(which, slot),
            fan_send.at[step, kind],
            fan_recv.at[slot, kind],
            peers[step],
        )

    keep_tok = pltpu.make_async_copy(tok, place(half, slot), local.at[0])

    @pl.when(jnp.logical_not(owned))
    def _():
        send_hop.start()

    @pl.when(owned)
    def _():
        for step in range(parts - 1):
            fan(step, 0).start()
        keep_tok.start()

    send_up = remote(up, up_all.at[lines(half)], up_send, up_recv, other_at)
    came_up = remote(up, up_all.at[lines(1 - half)], up_send, up_recv, other_at)
    send_up.start()
    keep_up = pltpu.make_async_copy(up, up_all.at[lines(half)], local.at[1])
    keep_up.start()
    load_first = pltpu.make_async_copy(first_old, first, local.at[2])
    load_first.start()
    load_second = pltpu.make_async_copy(second_old, second, local.at[3])
    load_second.start()

    @pl.when(jnp.logical_not(owned))
    def _():
        send_hop.wait_send()

    @pl.when(owned)
    def _():
        came_hop.wait_recv()
        for step in range(parts - 1):
            fan(step, 1).start()
        for step in range(parts - 1):
            fan(step, 0).wait_send()
            fan(step, 1).wait_send()
        keep_tok.wait()

    for index in range(per):

        @pl.when(part != half * per + index)
        def _(index=index):
            for kind, which in enumerate((half, 1 - half)):
                remote(
                    tok,
                    place(which, index),
                    fan_send.at[0, kind],
                    fan_recv.at[index, kind],
                    peers[0],
                ).wait_recv()

    turned[...] = tok_all[...].T
    square[...] = jnp.zeros_like(square)
    keep_up.wait()
    send_up.wait_send()
    came_up.wait_recv()
    bands = rows // BAND

    @pl.loop(0, bands * (cols // BAND))
    def _(index):
        high = pl.ds(pl.multiple_of(lax.rem(index, bands) * BAND, BAND), BAND)
        wide = pl.ds(pl.multiple_of(index // bands * BAND, BAND), BAND)
        product = jnp.dot(turned[high, :], up_all[:, wide], preferred_element_type=jnp.float32)
        grad[high, wide] = product
        square[...] += jnp.sum((product * product).reshape(BAND // 8, 8, BAND), axis=0)

    rank = half * parts + part
    sums = [
        remote(square, squares.at[rank], sum_send.at[index], sum_recv.at[rank], where)
        for index, where in enumerate(peers + across)
    ]
    for copy in sums:
        copy.start()
    squares[rank] = square[...]
    load_first.wait()
    load_second.wait()
    for copy in sums:
        copy.wait_send()
    for index in range(2 * parts):

        @pl.when(rank != index)
        def _(index=index):
            remote(
                square, squares.at[index], sum_send.at[0], sum_recv.at[index], peers[0]
            ).wait_recv()

    total = jnp.sum(squares[...], axis=0)
    total = jnp.sum(jnp.sum(total, axis=1, keepdims=True), axis=0, keepdims=True)
    clip = jnp.minimum(1.0, 1.0 / jnp.sqrt(total / (D * FF) + 1e-06))

    @pl.loop(0, rows // 16)
    def _(index):
        high = pl.ds(pl.multiple_of(index * 16, 16), 16)
        scaled = clip * grad[high, :]
        first[high, :] = (0.9 * first[high, :].astype(jnp.float32) + 0.1 * scaled).astype(
            jnp.bfloat16
        )

    keeps = [pltpu.make_async_copy(first, first_out, local.at[0])]
    keeps[0].start()

    @pl.loop(0, rows // 16)
    def _(index):
        high = pl.ds(pl.multiple_of(index * 16, 16), 16)
        scaled = clip * grad[high, :]
        second[high, :] = (
            0.95 * second[high, :].astype(jnp.float32) + 0.05 * scaled * scaled
        ).astype(jnp.bfloat16)

    start = 0
    for index, chunk in enumerate(chunks):
        size = chunk.shape[0]
        keep = pltpu.make_async_copy(second.at[pl.ds(start, size)], chunk, local.at[1 + index])
        keep.start()
        keeps.append(keep)
        start += size
    for keep in keeps:
        keep.wait()


def first_phase(tokens, upstream, first_moment, second_moment):
    count, feats = tokens.shape
    rows, cols = first_moment.shape
    parts = lax.axis_size("tensor")
    anywhere = pl.BlockSpec(memory_space=pl.ANY)
    dma = pltpu.SemaphoreType.DMA
    whole = jax.ShapeDtypeStruct((rows, cols), jnp.bfloat16)
    sizes = [rows * share // sum(SHARES) for share in SHARES]
    wide = max(2 * parts, 1 + len(SHARES), 4)
    outs = pl.pallas_call(
        first_kernel,
        in_specs=[anywhere] * 4,
        out_specs=(anywhere,) * (1 + len(sizes)),
        out_shape=(whole,)
        + tuple(jax.ShapeDtypeStruct((size, cols), jnp.bfloat16) for size in sizes),
        scratch_shapes=[
            pltpu.VMEM((2 * count, cols), jnp.bfloat16),
            pltpu.VMEM((2 * count, feats * (parts // 2)), jnp.bfloat16),
            pltpu.VMEM((feats * (parts // 2), 2 * count), jnp.bfloat16),
            pltpu.VMEM((rows, cols), jnp.float32),
            pltpu.VMEM((rows, cols), jnp.bfloat16),
            pltpu.VMEM((rows, cols), jnp.bfloat16),
            pltpu.VMEM((8, BAND), jnp.float32),
            pltpu.VMEM((2 * parts, 8, BAND), jnp.float32),
        ]
        + [dma(())] * 4
        + [dma((parts - 1, 2)), dma((parts // 2, 2)), dma((2 * parts - 1,)), dma((2, wide))],
        cost_estimate=pl.CostEstimate(
            flops=4 * count * rows * cols, bytes_accessed=20 * rows * cols, transcendentals=0
        ),
        compiler_params=pltpu.CompilerParams(
            collective_id=0, has_side_effects=True, vmem_limit_bytes=62 * 2**20
        ),
    )(tokens, upstream, first_moment, second_moment)
    return outs[0], outs[1:]


def gate_kernel(value, *refs):
    refs[-1][...] = value[...]


def gate(value, after):
    rows, cols = value.shape
    block = pl.BlockSpec((TILE, cols), lambda i: (i, 0))
    return pl.pallas_call(
        gate_kernel,
        grid=(rows // TILE,),
        in_specs=[block] + [pl.BlockSpec(memory_space=pl.ANY)] * len(after),
        out_specs=block,
        out_shape=jax.ShapeDtypeStruct((rows, cols), jnp.bfloat16),
        cost_estimate=pl.CostEstimate(
            flops=0, bytes_accessed=4 * rows * cols, transcendentals=0
        ),
        compiler_params=pltpu.CompilerParams(vmem_limit_bytes=60 * 2**20),
    )(value, *after)


def new_weights(old, first, second):
    old = old.astype(jnp.float32)
    first = first.astype(jnp.float32)
    second = second.astype(jnp.float32)
    update = first * (1.0 / FIX_ONE) / (jnp.sqrt(second * (1.0 / FIX_TWO)) + 1e-08)
    fresh = old - 0.05 * (update + 0.1 * old)
    return fresh.astype(jnp.bfloat16)


def mean(one, two):
    return (0.5 * (one.astype(jnp.float32) + two.astype(jnp.float32))).astype(jnp.bfloat16)


def mix_kernel(w, w2, m, m2, v, v2, *refs):
    out_w, out_m, out_v, done = refs[-4:]
    first, first2 = m[...], m2[...]
    second, second2 = v[...], v2[...]
    out_m[...] = mean(first, first2)
    out_v[...] = mean(second, second2)
    out_w[...] = mean(
        new_weights(w[...], first, second), new_weights(w2[...], first2, second2)
    )
    done[...] = jnp.zeros_like(done)


def mix_chunk(w, w2, m, m2, v, v2, held, start):
    rows, cols = v.shape
    first = start // TILE
    far = pl.BlockSpec((TILE, cols), lambda i: (first + i, 0))
    near = pl.BlockSpec((TILE, cols), lambda i: (i, 0))
    *outs, done = pl.pallas_call(
        mix_kernel,
        grid=(rows // TILE,),
        in_specs=[far, far, far, far, near, near]
        + [pl.BlockSpec(memory_space=pl.ANY)] * len(held),
        out_specs=(far, far, far, pl.BlockSpec((8, 128), lambda i: (0, 0))),
        out_shape=(jax.ShapeDtypeStruct(w.shape, jnp.bfloat16),) * 3
        + (jax.ShapeDtypeStruct((8, 128), jnp.float32),),
        input_output_aliases={6 + i: i for i in range(len(held))},
        cost_estimate=pl.CostEstimate(
            flops=30 * rows * cols, bytes_accessed=18 * rows * cols, transcendentals=4 * rows * cols
        ),
        compiler_params=pltpu.CompilerParams(vmem_limit_bytes=60 * 2**20),
    )(w, w2, m, m2, v, v2, *held)
    return outs, done


def body(tokens, grad_out, weights, first_moment, second_moment):
    bit = lax.axis_size("replica").bit_length() - 2
    weights = weights[0]
    weights2 = partner(weights, "replica", bit)
    first, chunks = first_phase(tokens[0], grad_out[0], first_moment[0], second_moment[0])
    first2 = partner(first, "replica", bit)
    arrived, mixed, outs, start = [], [], (), 0
    waits = (weights2, 0, first2, 1, 2, 3, 4)
    for index, second in enumerate(chunks):
        wait = waits[index]
        after = [arrived[wait] if isinstance(wait, int) else wait]
        if index >= 3:
            after.append(mixed[index - 3])
        second = gate(second, after)
        second2 = partner(second, "replica", bit)
        arrived.append(second2)
        outs, done = mix_chunk(weights, weights2, first, first2, second, second2, outs, start)
        mixed.append(done)
        start += second.shape[0]
    return tuple(out[None] for out in outs)


def solution(mesh):
    placed = P("replica", "dp", "tensor")
    return jax.shard_map(
        body,
        mesh=mesh,
        in_specs=(placed,) * 5,
        out_specs=(placed,) * 3,
        check_vma=False,
    )
```
